128 devices in a mesh: row: 32 (over y, x, core), col: 4 (over z).
Axes of the slice: x: 4, y: 4, z: 4, core: 2. Of those that a mesh axis runs over, the one named last changes fastest.
Arguments:
- integrals: bfloat16 [32768, 4096], P('row', 'col'), may hold values from -6 to 6
- amplitudes: bfloat16 [4096, 6144], P('row', 'col'), may hold values from -0.25 to 0.25
- screen: int32 [32, 48], P('row', 'col'), may hold values from 0 to 1, as said below
- next_owner: int32 [256], replicated, may hold values from 0 to 31, as said below
Outputs:
- regrouped: bfloat16 [32768, 6144], P('row', 'col')
The draws below stay inside these ranges and needn't reach their ends.
Inputs may be any that keep to these rules, and one draw needn't show every extreme that they name: In each aligned block of 1 x 12 tiles of screen (one device's block), between 1 and 2 entries are 1; some block holds exactly 2. next_owner[p * 8 + s] equals p XOR m_s, where m_s (0 to 31) depends only on s.
All inputs are finite; a program needn't handle non-finite values.
Results may differ from the reference program's by a relative error of at most 0.001.
Values may be sent and summed in bfloat16 or wider, within the bound.
No kernel may reach another device: no remote copies, remote signals or barrier semaphores. Data moves between devices by JAX's collectives and lax.ppermute only.
A program may use at most 128 MiB of HBM per device.

```python
import jax
import jax.numpy as jnp
from jax import lax

TILE = 128
ROW_TILES = 8
COL_TILES = 12
K_TILES = 1
CAP = 2
ROWS_ALL = 32768
DEPTH = 4096
WIDTH = 6144
N_ROW = 32
N_COL = 4


def draw_screen(key, part):
    key = jax.random.fold_in(key, 7)
    block_count = N_ROW * N_COL
    cell_count = K_TILES * COL_TILES
    key_counts, key_full, key_order = jax.random.split(key, 3)
    counts = jax.random.randint(key_counts, (block_count,), 1, CAP + 1)
    fullest = jax.random.randint(key_full, (), 0, block_count)
    counts = jnp.where(jnp.arange(block_count) == fullest, CAP, counts)
    block_keys = jax.random.split(key_order, block_count)
    orders = jax.vmap(lambda single: jax.random.permutation(single, cell_count))(block_keys)
    flags = (orders < counts[:, None]).astype(jnp.int32)
    flags = flags.reshape(N_ROW, N_COL, K_TILES, COL_TILES).transpose(0, 2, 1, 3)
    return flags.reshape(N_ROW * K_TILES, N_COL * COL_TILES)


def draw_next_owner(key, part):
    key = jax.random.fold_in(key, 11)
    moves = jax.random.randint(key, (ROW_TILES,), 0, N_ROW)
    owners = jnp.bitwise_xor(jnp.arange(N_ROW, dtype=jnp.int32)[:, None], moves[None, :].astype(jnp.int32))
    return owners.reshape(N_ROW * ROW_TILES).astype(jnp.int32)


def shard_levels(stream_key, dims, cuts, smallest, high):
    level = 1.0
    for dim, blocks in cuts:
        steps = jax.random.uniform(jax.random.fold_in(jax.random.fold_in(stream_key, 6), dim), (blocks,), jnp.float32, smallest / len(cuts), high / len(cuts))
        level = level * jnp.repeat(jnp.exp(steps), dims[dim] // blocks).reshape((-1,) + (1,) * (len(dims) - 1 - dim))
    return level


def scatter_about(rng, dims, scale, bound, shards=(), held_as=jnp.bfloat16):
    drawn = jax.random.normal(rng, dims, jnp.float32) * scale
    if len(shards) > 0:
        drawn = shard_levels(rng, dims, shards, -0.22, 0.18) * drawn
    return jnp.clip(drawn, min=-bound, max=bound).astype(held_as)


def setup_inputs(seed: int = 0) -> dict:
    splits = jax.random.split(jax.random.key(seed), 5)
    return {
        "integrals": scatter_about(splits[0], (ROWS_ALL, DEPTH), 1.0, 6.0, ((0, 32), (1, 4))),
        "amplitudes": scatter_about(splits[1], (DEPTH, WIDTH), (max(TILE, TILE * N_ROW * (CAP + 1) // (2 * COL_TILES))) ** -0.5, 0.25, ((0, 32), (1, 4))),
        "screen": draw_screen(jax.random.fold_in(splits[4], 71), 0),
        "next_owner": draw_next_owner(jax.random.fold_in(splits[4], 71), 0),
    }


def reference(integrals, amplitudes, screen, next_owner):
    row_count = integrals.shape[0]
    col_width = amplitudes.shape[1]
    depth_tiles = screen.shape[0]
    width_tiles = screen.shape[1]
    order = jnp.arange(depth_tiles * width_tiles, dtype=jnp.int32)

    def step(total, position):
        depth_at = (position // width_tiles).astype(jnp.int32)
        width_at = (position % width_tiles).astype(jnp.int32)

        def add_tile(carried):
            left_block = lax.dynamic_slice_in_dim(integrals, depth_at * TILE, TILE, 1)
            right_block = lax.dynamic_slice(amplitudes, (depth_at * TILE, width_at * TILE), (TILE, TILE))
            before = lax.dynamic_slice_in_dim(carried, width_at * TILE, TILE, 1)
            after = before + jnp.dot(left_block, right_block, preferred_element_type=jnp.float32)
            return lax.dynamic_update_slice_in_dim(carried, after, width_at * TILE, 1)

        def keep_tile(carried):
            return carried

        return lax.cond(screen[depth_at, width_at] == 1, add_tile, keep_tile, total), None

    start_total = jnp.zeros((row_count, col_width), jnp.float32)
    product, unused = lax.scan(step, start_total, order)
    residual = product.astype(jnp.bfloat16)
    row_tiles_all = row_count // TILE
    tiled = residual.reshape(row_tiles_all, TILE, col_width)
    slot_index = jnp.arange(row_tiles_all, dtype=jnp.int32) % ROW_TILES
    new_place = (next_owner.astype(jnp.int32) * ROW_TILES + slot_index).astype(jnp.int32)
    moved = jnp.zeros_like(tiled).at[new_place].set(tiled)
    return moved.reshape(row_count, col_width)
```

```python
import functools

import jax
import jax.numpy as jnp
from jax import lax
from jax.experimental import pallas as pl
from jax.experimental.pallas import tpu as pltpu
from jax.sharding import PartitionSpec as P

TILE = 128
SLOTS = 8
GROUPS = ((0, 2), (2, 4), (4, 6), (6, 8))
X1, X3, Y1, Y3, CORE = 2, 6, 8, 24, 1
AXES = ("row", "col")


def exchange(value, masks):
    pairs = [(p, p ^ masks[p & 1]) for p in range(lax.axis_size("row"))]
    return lax.ppermute(value, "row", pairs)


def turn(value):
    rows, cols = lax.axis_size("row"), lax.axis_size("col")
    pairs = []
    for p in range(rows):
        step = 1 if p & 1 == 0 else -1
        for c in range(cols):
            pairs.append((p * cols + c, p * cols + (c + step) % cols))
    return lax.ppermute(value, AXES, pairs)


def need(moves, mask):
    if mask == CORE:
        return moves & 1 == 1
    shift = 1 if mask in (X1, X3) else 3
    low, high = moves >> shift & 1, moves >> (shift + 1) & 1
    return (high if mask in (X3, Y3) else low ^ high) == 1


def step(value, moves, masks, core):
    partner = exchange(value, masks)
    if masks[0] == masks[1]:
        flags = need(moves, masks[0])
    else:
        flags = jnp.where(core == 0, need(moves, masks[0]), need(moves, masks[1]))
    return jnp.where(flags[:, None, None], partner, value)


def regroup(value, moves, core):
    value = step(value, moves, (CORE, CORE), core)
    half = value.shape[0] // 2
    parts = [value[:half], value[half:]]
    order_x = [(X1, X3), (X3, X1)]
    order_y = [(Y1, Y3), (Y3, Y1)]
    orders = [order_x + order_y, order_y + order_x]
    cuts = [moves[:half], moves[half:]]
    for at in range(4):
        parts = [step(parts[i], cuts[i], orders[i][at], core) for i in range(2)]
    return jnp.concatenate(parts, axis=0)


def gather_tiles(packed, core):
    held = packed[None]
    for masks in ((X1, X3), (X3, X1), (Y1, Y3), (Y3, Y1)):
        held = jnp.concatenate([held, exchange(held, masks)], axis=0)
    return jnp.concatenate([held, exchange(held, (CORE, CORE))], axis=0)


def tile_order(me):
    k = jnp.arange(32, dtype=jnp.int32)
    delta = k ^ me
    other = delta & 1
    core = k & 1
    bit = [delta >> i & 1 for i in range(5)]
    x1, x3, y1, y3 = bit[1] ^ bit[2], bit[2], bit[3] ^ bit[4], bit[4]
    first = jnp.where(core == 0, x1 + 2 * x3 + 4 * y1 + 8 * y3, x3 + 2 * x1 + 4 * y3 + 8 * y1)
    return (first + 16 * other).astype(jnp.int32)


def product_kernel(at_ref, place_ref, base_ref, x0, x1, x2, x3, tiles_ref, *rest):
    out_ref, total = rest[-2:]
    total[...] = jnp.zeros_like(total)
    for j, x_ref in enumerate((x0, x1, x2, x3)):
        for kk in range(8):
            k = base_ref[j] * 8 + kk
            part = jnp.dot(
                x_ref[:, kk * TILE : (kk + 1) * TILE],
                tiles_ref[at_ref[k], :TILE, :],
                preferred_element_type=jnp.float32,
            )
            for i in range(2):
                where = pl.ds(pl.multiple_of(place_ref[2 * k + i] * TILE, TILE), TILE)
                total[:, where] += part[:, i * TILE : (i + 1) * TILE]
    out_ref[...] = total[...].astype(out_ref.dtype)


def product(blocks, tiles, at, place, base, out, first, rows_all):
    rows = blocks[0].shape[0]
    width = 12 * TILE
    where = first // rows
    in_specs = [pl.BlockSpec((rows, 1024), lambda i, *_: (0, 0))] * 4
    in_specs.append(pl.BlockSpec(tiles.shape, lambda i, *_: (0, 0, 0)))
    args = list(blocks) + [tiles]
    aliases = {}
    if out is not None:
        in_specs.append(pl.BlockSpec(memory_space=pl.ANY))
        args.append(out)
        aliases = {8: 0}
    return pl.pallas_call(
        product_kernel,
        grid_spec=pltpu.PrefetchScalarGridSpec(
            num_scalar_prefetch=3,
            grid=(1,),
            in_specs=in_specs,
            out_specs=pl.BlockSpec((rows, width), lambda i, *_: (where, 0)),
            scratch_shapes=[pltpu.VMEM((rows, width), jnp.float32)],
        ),
        out_shape=jax.ShapeDtypeStruct((rows_all, width), jnp.bfloat16),
        input_output_aliases=aliases,
        compiler_params=pltpu.CompilerParams(vmem_limit_bytes=40 * 2**20),
        cost_estimate=pl.CostEstimate(
            flops=rows * 4096 * 256 * 4, bytes_accessed=rows * 11264 + 2**21, transcendentals=0
        ),
    )(at, place, base, *args)


def body(integrals, amplitudes, screen, next_owner):
    me = lax.axis_index("row").astype(jnp.int32)
    col = lax.axis_index("col").astype(jnp.int32)
    core = me & 1
    moves = next_owner[:SLOTS]

    flags = screen[0] == 1
    spots = jnp.arange(12, dtype=jnp.int32)
    first = jnp.min(jnp.where(flags, spots, 11))
    second = jnp.max(jnp.where(flags, spots, 0))
    both = first != second
    one = lax.dynamic_slice(amplitudes, (0, first * TILE), (TILE, TILE))
    two = lax.dynamic_slice(amplitudes, (0, second * TILE), (TILE, TILE))
    two = jnp.where(both, two, jnp.zeros_like(two))
    live = jnp.concatenate([one, two], axis=1)
    spot = jnp.concatenate(
        [jnp.full((16, TILE), first, jnp.int32), jnp.full((16, TILE), second, jnp.int32)], axis=1
    ).astype(jnp.bfloat16)
    tiles = gather_tiles(jnp.concatenate([live, spot], axis=0), core)
    at = tile_order(me)
    place = tiles[:, TILE, :].reshape(32, 2, TILE)[:, :, 0].astype(jnp.int32)
    place = place[at].reshape(64)
    sign = 1 - 2 * core
    base = (col - sign * jnp.arange(4, dtype=jnp.int32)) & 3

    slots = integrals.reshape(SLOTS, TILE, 1024)
    out = None
    for low, high in GROUPS:
        held = regroup(slots[low:high], moves[low:high], core).reshape((high - low) * TILE, 1024)
        blocks = [held]
        for _ in range(3):
            blocks.append(turn(blocks[-1]))
        out = product(blocks, tiles, at, place, base, out, low * TILE, 1024)
    return out


def solution(mesh):
    placed = (P("row", "col"), P("row", "col"), P("row", "col"), P())
    return jax.shard_map(
        body, mesh=mesh, in_specs=placed, out_specs=P("row", "col"), check_vma=False
    )
```

```python
import functools

import jax
import jax.numpy as jnp
import numpy as np
from jax import lax
from jax.experimental import pallas as pl
from jax.experimental.pallas import tpu as pltpu
from jax.sharding import PartitionSpec as P

TILE = 128
SLOTS = 8
DEPTH = 1024
WIDTH = 1536
CORE = (1, 1)
X_A, X_B, Y_A, Y_B = (2, 6), (6, 2), (8, 24), (24, 8)
STEPS = (CORE, X_A, X_B, Y_A, Y_B)
FUNCTIONAL = {1: 1, 2: 6, 6: 4, 8: 24, 24: 16}
GATHER = (X_A, X_B, Y_A, Y_B)
AXES = ("row", "col")


def exchange(value, masks):
    pairs = [(p, p ^ masks[p & 1]) for p in range(lax.axis_size("row"))]
    return lax.ppermute(value, "row", pairs)


def turn(value):
    rows, cols = lax.axis_size("row"), lax.axis_size("col")
    pairs = []
    for p in range(rows):
        step = 1 if p & 1 == 0 else -1
        for c in range(cols):
            pairs.append((p * cols + c, p * cols + (c + step) % cols))
    return lax.ppermute(value, AXES, pairs)


def choose(flags, masks, low, high, partner, mine):
    taken = flags[STEPS.index(masks), low:high] == 1
    return jnp.where(taken[:, None, None], partner, mine)


def pack_kernel(screen_ref, amplitudes_ref, out_ref):
    first = jnp.int32(11)
    second = jnp.int32(0)
    for j in range(12):
        live = screen_ref[0, j] == 1
        first = jnp.where(live, jnp.minimum(first, j), first)
        second = jnp.where(live, jnp.maximum(second, j), second)
    one = amplitudes_ref[:, pl.ds(pl.multiple_of(first * TILE, TILE), TILE)]
    two = amplitudes_ref[:, pl.ds(pl.multiple_of(second * TILE, TILE), TILE)]
    out_ref[0, :TILE, :TILE] = one
    out_ref[0, :TILE, TILE:] = jnp.where(first != second, two, jnp.zeros_like(two))
    side = lax.broadcasted_iota(jnp.int32, (16, 2 * TILE), 1) < TILE
    out_ref[0, TILE:, :] = jnp.where(side, first, second).astype(jnp.float32).astype(jnp.bfloat16)


def pack(amplitudes, screen):
    return pl.pallas_call(
        pack_kernel,
        in_specs=[pl.BlockSpec(memory_space=pltpu.SMEM), pl.BlockSpec(memory_space=pltpu.VMEM)],
        out_specs=pl.BlockSpec(memory_space=pltpu.VMEM),
        out_shape=jax.ShapeDtypeStruct((1, TILE + 16, 2 * TILE), jnp.bfloat16),
        cost_estimate=pl.CostEstimate(flops=1, bytes_accessed=1, transcendentals=0),
    )(screen, amplitudes)


def order_table():
    table = np.zeros((32, 32), np.int32)
    for me in range(32):
        for k in range(32):
            delta = k ^ me
            at = 16 * (delta & 1)
            for i, masks in enumerate(GATHER):
                at += (bin(delta & FUNCTIONAL[masks[k & 1]]).count("1") & 1) << i
            table[me, k] = at
    return table


def product_kernel(first, at_ref, place_ref, base_ref, *refs):
    *sources, tiles_hbm = refs[:5]
    out_hbm, x, tiles, total, out, sems = refs[-6:]
    rows = total.shape[0]
    loads = [pltpu.make_async_copy(tiles_hbm, tiles, sems.at[4])]
    loads += [pltpu.make_async_copy(sources[j], x.at[j], sems.at[j]) for j in range(4)]
    for load in loads:
        load.start()
    total[...] = jnp.zeros_like(total)
    loads[0].wait()
    for j in range(4):
        loads[j + 1].wait()

        for kk in range(8):
            at = at_ref[0, base_ref[j] * 8 + kk]
            part = jnp.dot(
                x[j, :, kk * TILE : (kk + 1) * TILE],
                tiles[at, :TILE, :],
                preferred_element_type=jnp.float32,
            )
            for i in range(2):
                where = pl.ds(pl.multiple_of(place_ref[2 * at + i] * TILE, TILE), TILE)
                total[:, where] += part[:, i * TILE : (i + 1) * TILE]

    out[...] = total[...].astype(out.dtype)
    store = pltpu.make_async_copy(out, out_hbm.at[pl.ds(first, rows)], sems.at[5])
    store.start()
    store.wait()


def product(blocks, tiles, at, place, base, out=None, first=0, rows_all=None):
    rows = blocks[0].shape[0]
    rows_all = rows_all or rows
    args = list(blocks) + [tiles]
    aliases = {}
    if out is not None:
        args.append(out)
        aliases = {8: 0}
    return pl.pallas_call(
        functools.partial(product_kernel, first),
        grid_spec=pltpu.PrefetchScalarGridSpec(
            num_scalar_prefetch=3,
            grid=(1,),
            in_specs=[pl.BlockSpec(memory_space=pl.ANY)] * len(args),
            out_specs=pl.BlockSpec(memory_space=pl.ANY),
            scratch_shapes=[
                pltpu.VMEM((4, rows, DEPTH), jnp.bfloat16),
                pltpu.VMEM(tiles.shape, jnp.bfloat16),
                pltpu.VMEM((rows, WIDTH), jnp.float32),
                pltpu.VMEM((rows, WIDTH), jnp.bfloat16),
                pltpu.SemaphoreType.DMA((6,)),
            ],
        ),
        out_shape=jax.ShapeDtypeStruct((rows_all, WIDTH), jnp.bfloat16),
        input_output_aliases=aliases,
        compiler_params=pltpu.CompilerParams(vmem_limit_bytes=24 * 2**20),
        cost_estimate=pl.CostEstimate(flops=1, bytes_accessed=1, transcendentals=0),
    )(at, place, base, *args)


class Sequence:
    def __init__(self, token):
        self.token = token

    def tied(self, *values):
        return lax.optimization_barrier((*values, self.token))[: len(values)]

    def after(self, value):
        return self.tied(value)[0]

    def done(self, value):
        self.token = self.after(value)
        return self.token


PAIRS = ((0, 2), (2, 4), (4, 6), (6, 8))
PATHS = (
    (X_A, X_B, Y_A, Y_B),
    (Y_A, X_A, Y_B, X_B),
    (Y_A, X_A, X_B, Y_B),
    (X_A, Y_A, Y_B, X_B),
)


def body(integrals, amplitudes, screen, next_owner):
    me = lax.axis_index("row").astype(jnp.int32)
    col = lax.axis_index("col").astype(jnp.int32)
    core = me & 1
    slots = integrals.reshape(SLOTS, TILE, DEPTH)

    functional = [jnp.asarray([[FUNCTIONAL[m[c]]] for m in STEPS], jnp.int32) for c in range(2)]
    value = next_owner[None, :SLOTS] & jnp.where(core == 0, functional[0], functional[1])
    value = value ^ value >> 4
    value = value ^ value >> 2
    value = value ^ value >> 1
    flags = value & 1
    at = lax.dynamic_slice(jnp.asarray(order_table()), (me, 0), (1, 32))
    sign = 1 - 2 * core
    base = (col - sign * jnp.arange(4, dtype=jnp.int32)) & 3
    flags, at, base = lax.optimization_barrier((flags, at, base))

    seq = Sequence(next_owner)

    class Moving:
        def __init__(self, value, cut, order):
            self.value, self.cut, self.order, self.at = value, cut, order, 0

        def send(self):
            self.value = seq.after(self.value)
            self.partner = exchange(self.value, self.order[self.at])

        def take(self):
            partner, mine = seq.tied(self.partner, self.value)
            self.value = seq.done(choose(flags, self.order[self.at], *self.cut, partner, mine))
            self.at += 1

    class Ring:
        def __init__(self, value):
            self.blocks = [value]

        def send(self):
            self.blocks.append(turn(seq.after(self.blocks[-1])))

        def take(self):
            self.blocks[-1] = seq.done(self.blocks[-1])

    class Tiles:
        def __init__(self, value):
            self.value, self.at = value, 0

        def send(self):
            self.value = seq.after(self.value)
            self.partner = exchange(self.value, (*GATHER, CORE)[self.at])
            self.at += 1

        def take(self):
            partner, mine = seq.tied(self.partner, self.value)
            self.value = seq.done(jnp.concatenate([mine, partner], axis=0))

    class Swapped:
        def __init__(self):
            self.partner = exchange(slots, CORE)

        def pair(self, low, high):
            other, mine = seq.tied(self.partner, slots)
            return seq.done(choose(flags, CORE, low, high, other[low:high], mine[low:high]))

    def times(ring):
        live = tiles.value
        place = live[:, TILE, :].reshape(32, 2, TILE)[:, :, 0].astype(jnp.int32).reshape(64)
        return product(ring.blocks, live, at, place, base)

    def finish(ring, out, low):
        live = tiles.value
        place = live[:, TILE, :].reshape(32, 2, TILE)[:, :, 0].astype(jnp.int32).reshape(64)
        return product(ring.blocks, live, at, place, base, out, low * TILE, SLOTS * TILE)

    early, late, rings = [None] * 2, [None] * 2, [None] * 4
    swapped = Swapped()
    tiles = Tiles(seq.done(pack(amplitudes, screen)))
    tiles.send()
    rings[3] = Ring(swapped.pair(*PAIRS[3]).reshape(2 * TILE, DEPTH))
    tiles.take()
    rings[3].send()
    tiles.send()
    rings[2] = Ring(swapped.pair(*PAIRS[2]).reshape(2 * TILE, DEPTH))
    early[0] = Moving(swapped.pair(*PAIRS[0]), PAIRS[0], PATHS[0])
    early[0].send()
    rings[2].send()
    early[1] = Moving(swapped.pair(*PAIRS[1]), PAIRS[1], PATHS[1])
    tiles.take()
    tiles.send()
    early[1].send()
    rings[3].take()
    rings[3].send()
    early[0].take()
    early[0].send()
    tiles.take()
    tiles.send()
    rings[2].take()
    rings[2].send()
    early[1].take()
    early[1].send()
    rings[3].take()
    rings[3].send()
    early[0].take()
    early[0].send()
    tiles.take()
    tiles.send()
    rings[2].take()
    rings[2].send()
    early[1].take()
    early[1].send()
    tiles.take()
    rings[3].take()
    value = seq.done(times(rings[3])).reshape(2, TILE, WIDTH)
    late[1] = Moving(value, PAIRS[3], PATHS[3])
    early[0].take()
    early[0].send()
    late[1].send()
    rings[2].take()
    value = seq.done(times(rings[2])).reshape(2, TILE, WIDTH)
    late[0] = Moving(value, PAIRS[2], PATHS[2])
    late[0].send()
    early[1].take()
    early[1].send()
    early[0].take()
    rings[0] = Ring(early[0].value.reshape(2 * TILE, DEPTH))
    rings[0].send()
    late[1].take()
    late[1].send()
    late[0].take()
    late[0].send()
    early[1].take()
    rings[1] = Ring(early[1].value.reshape(2 * TILE, DEPTH))
    rings[1].send()
    rings[0].take()
    rings[0].send()
    late[1].take()
    late[1].send()
    late[0].take()
    late[0].send()
    rings[1].take()
    rings[1].send()
    rings[0].take()
    rings[0].send()
    late[1].take()
    late[1].send()
    rings[1].take()
    rings[1].send()
    late[0].take()
    late[0].send()
    rings[0].take()
    out = seq.done(finish(rings[0], None, PAIRS[0][0]))
    late[1].take()
    rings[1].take()
    out = seq.done(finish(rings[1], out, PAIRS[1][0]))
    late[0].take()

    for part, (low, _) in zip(late, PAIRS[2:]):
        out = lax.dynamic_update_slice(out, part.value.reshape(2 * TILE, WIDTH), (low * TILE, 0))
    return out


def solution(mesh):
    placed = (P("row", "col"), P("row", "col"), P("row", "col"), P())
    return jax.shard_map(
        body, mesh=mesh, in_specs=placed, out_specs=P("row", "col"), check_vma=False
    )
```

```python
import functools

import jax
import jax.numpy as jnp
import numpy as np
from jax import lax
from jax.experimental import pallas as pl
from jax.experimental.pallas import tpu as pltpu
from jax.sharding import PartitionSpec as P

TILE = 128
SLOTS = 8
DEPTH = 1024
WIDTH = 1536
CORE = (1, 1)
X_A, X_B, Y_A, Y_B = (2, 6), (6, 2), (8, 24), (24, 8)
STEPS = (CORE, X_A, X_B, Y_A, Y_B)
FUNCTIONAL = {1: 1, 2: 6, 6: 4, 8: 24, 24: 16}
GATHER = (X_A, X_B, Y_A, Y_B)
AXES = ("row", "col")


def exchange(value, masks):
    pairs = [(p, p ^ masks[p & 1]) for p in range(lax.axis_size("row"))]
    return lax.ppermute(value, "row", pairs)


def turn(value):
    rows, cols = lax.axis_size("row"), lax.axis_size("col")
    pairs = []
    for p in range(rows):
        step = 1 if p & 1 == 0 else -1
        for c in range(cols):
            pairs.append((p * cols + c, p * cols + (c + step) % cols))
    return lax.ppermute(value, AXES, pairs)


def choose(flags, masks, low, high, partner, mine):
    taken = flags[STEPS.index(masks), low:high] == 1
    return jnp.where(taken[:, None, None], partner, mine)


def pack_kernel(screen_ref, amplitudes_ref, out_ref):
    first = jnp.int32(11)
    second = jnp.int32(0)
    for j in range(12):
        live = screen_ref[0, j] == 1
        first = jnp.where(live, jnp.minimum(first, j), first)
        second = jnp.where(live, jnp.maximum(second, j), second)
    one = amplitudes_ref[:, pl.ds(pl.multiple_of(first * TILE, TILE), TILE)]
    two = amplitudes_ref[:, pl.ds(pl.multiple_of(second * TILE, TILE), TILE)]
    out_ref[0, :TILE, :TILE] = one
    out_ref[0, :TILE, TILE:] = jnp.where(first != second, two, jnp.zeros_like(two))
    side = lax.broadcasted_iota(jnp.int32, (16, 2 * TILE), 1) < TILE
    out_ref[0, TILE:, :] = jnp.where(side, first, second).astype(jnp.float32).astype(jnp.bfloat16)


def pack(amplitudes, screen):
    return pl.pallas_call(
        pack_kernel,
        in_specs=[pl.BlockSpec(memory_space=pltpu.SMEM), pl.BlockSpec(memory_space=pltpu.VMEM)],
        out_specs=pl.BlockSpec(memory_space=pltpu.VMEM),
        out_shape=jax.ShapeDtypeStruct((1, TILE + 16, 2 * TILE), jnp.bfloat16),
        cost_estimate=pl.CostEstimate(flops=1, bytes_accessed=1, transcendentals=0),
    )(screen, amplitudes)


def order_table():
    table = np.zeros((32, 32), np.int32)
    for me in range(32):
        for k in range(32):
            delta = k ^ me
            at = 16 * (delta & 1)
            for i, masks in enumerate(GATHER):
                at += (bin(delta & FUNCTIONAL[masks[k & 1]]).count("1") & 1) << i
            table[me, k] = at
    return table


def product_kernel(first, at_ref, place_ref, base_ref, *refs):
    *sources, tiles_hbm = refs[:5]
    out_hbm, x, tiles, total, out, sems = refs[-6:]
    rows = total.shape[0]
    loads = [pltpu.make_async_copy(tiles_hbm, tiles, sems.at[4])]
    loads += [pltpu.make_async_copy(sources[j], x.at[j], sems.at[j]) for j in range(4)]
    for load in loads:
        load.start()
    total[...] = jnp.zeros_like(total)
    loads[0].wait()
    for j in range(4):
        loads[j + 1].wait()

        for kk in range(8):
            at = at_ref[0, base_ref[j] * 8 + kk]
            part = jnp.dot(
                x[j, :, kk * TILE : (kk + 1) * TILE],
                tiles[at, :TILE, :],
                preferred_element_type=jnp.float32,
            )
            for i in range(2):
                where = pl.ds(pl.multiple_of(place_ref[2 * at + i] * TILE, TILE), TILE)
                total[:, where] += part[:, i * TILE : (i + 1) * TILE]

    out[...] = total[...].astype(out.dtype)
    store = pltpu.make_async_copy(out, out_hbm.at[pl.ds(first, rows)], sems.at[5])
    store.start()
    store.wait()


def product(blocks, tiles, at, place, base, out=None, first=0, rows_all=None):
    rows = blocks[0].shape[0]
    rows_all = rows_all or rows
    args = list(blocks) + [tiles]
    aliases = {}
    if out is not None:
        args.append(out)
        aliases = {8: 0}
    return pl.pallas_call(
        functools.partial(product_kernel, first),
        grid_spec=pltpu.PrefetchScalarGridSpec(
            num_scalar_prefetch=3,
            grid=(1,),
            in_specs=[pl.BlockSpec(memory_space=pl.ANY)] * len(args),
            out_specs=pl.BlockSpec(memory_space=pl.ANY),
            scratch_shapes=[
                pltpu.VMEM((4, rows, DEPTH), jnp.bfloat16),
                pltpu.VMEM(tiles.shape, jnp.bfloat16),
                pltpu.VMEM((rows, WIDTH), jnp.float32),
                pltpu.VMEM((rows, WIDTH), jnp.bfloat16),
                pltpu.SemaphoreType.DMA((6,)),
            ],
        ),
        out_shape=jax.ShapeDtypeStruct((rows_all, WIDTH), jnp.bfloat16),
        input_output_aliases=aliases,
        compiler_params=pltpu.CompilerParams(vmem_limit_bytes=16 * 2**20),
        cost_estimate=pl.CostEstimate(flops=1, bytes_accessed=1, transcendentals=0),
    )(at, place, base, *args)


class Sequence:
    def __init__(self, token):
        self.token = token

    def tied(self, *values):
        return lax.optimization_barrier((*values, self.token))[: len(values)]

    def after(self, value):
        return self.tied(value)[0]

    def done(self, value):
        self.token = self.after(value)
        return self.token


SPANS = ((0, 2), (2, 4), (4, 6), (6, 8))
PATHS = (
    (Y_A, Y_B, X_A, X_B),
    (X_A, X_B, Y_A, Y_B),
    (X_A, Y_A, Y_B, X_B),
    (Y_A, Y_B, X_A, X_B),
)


def body(integrals, amplitudes, screen, next_owner):
    me = lax.axis_index("row").astype(jnp.int32)
    col = lax.axis_index("col").astype(jnp.int32)
    core = me & 1
    slots = integrals.reshape(SLOTS, TILE, DEPTH)

    functional = [jnp.asarray([[FUNCTIONAL[m[c]]] for m in STEPS], jnp.int32) for c in range(2)]
    value = next_owner[None, :SLOTS] & jnp.where(core == 0, functional[0], functional[1])
    value = value ^ value >> 4
    value = value ^ value >> 2
    value = value ^ value >> 1
    flags = value & 1
    at = lax.dynamic_slice(jnp.asarray(order_table()), (me, 0), (1, 32))
    sign = 1 - 2 * core
    base = (col - sign * jnp.arange(4, dtype=jnp.int32)) & 3
    flags, at, base = lax.optimization_barrier((flags, at, base))

    seq = Sequence(next_owner)

    class Moving:
        def __init__(self, value, cut, order):
            self.value, self.cut, self.order, self.at = value, cut, order, 0

        def send(self):
            self.value = seq.after(self.value)
            self.partner = exchange(self.value, self.order[self.at])

        def take(self):
            partner, mine = seq.tied(self.partner, self.value)
            self.value = seq.done(choose(flags, self.order[self.at], *self.cut, partner, mine))
            self.at += 1

    class Ring:
        def __init__(self, value):
            self.blocks = [value]

        def send(self):
            self.blocks.append(turn(seq.after(self.blocks[-1])))

        def take(self):
            self.blocks[-1] = seq.done(self.blocks[-1])

    class Tiles:
        def __init__(self, value):
            self.value, self.at = value, 0

        def send(self):
            self.value = seq.after(self.value)
            self.partner = exchange(self.value, (*GATHER, CORE)[self.at])
            self.at += 1

        def take(self):
            partner, mine = seq.tied(self.partner, self.value)
            self.value = seq.done(jnp.concatenate([mine, partner], axis=0))

    swapped = exchange(slots, CORE)

    def group(number):
        low, high = SPANS[number]
        other, mine = seq.tied(swapped, slots)
        value = seq.done(choose(flags, CORE, low, high, other[low:high], mine[low:high]))
        return Moving(value, SPANS[number], PATHS[number])

    def ring(moving):
        return Ring(moving.value.reshape(-1, DEPTH))

    def times(blocks, *place_in):
        live = tiles.value
        place = live[:, TILE, :].reshape(32, 2, TILE)[:, :, 0].astype(jnp.int32).reshape(64)
        return seq.done(product(blocks, live, at, place, base, *place_in))

    def onward(moving, blocks):
        value = times(blocks).reshape(-1, TILE, WIDTH)
        later = Moving(value, moving.cut, moving.order)
        later.at = moving.at
        return later

    moving, rings = [None] * 4, [None] * 4
    tiles = Tiles(seq.done(pack(amplitudes, screen)))
    tiles.send()
    moving[0] = group(0)
    moving[3] = group(3)
    moving[3].send()
    tiles.take()
    tiles.send()
    moving[1] = group(1)
    moving[1].send()
    rings[0] = ring(moving[0])
    rings[0].send()
    moving[2] = group(2)
    moving[2].send()
    tiles.take()
    tiles.send()
    moving[3].take()
    moving[3].send()
    moving[1].take()
    moving[1].send()
    rings[0].take()
    rings[0].send()
    tiles.take()
    tiles.send()
    moving[2].take()
    moving[2].send()
    moving[3].take()
    moving[3].send()
    moving[1].take()
    rings[0].take()
    rings[0].send()
    rings[1] = ring(moving[1])
    rings[1].send()
    tiles.take()
    tiles.send()
    moving[3].take()
    moving[3].send()
    tiles.take()
    moving[2].take()
    moving[2].send()
    rings[0].take()
    rings[1].take()
    moving[0] = onward(moving[0], rings[0].blocks)
    moving[0].send()
    rings[1].send()
    moving[3].take()
    rings[3] = ring(moving[3])
    rings[3].send()
    moving[2].take()
    moving[2].send()
    rings[1].take()
    rings[1].send()
    moving[0].take()
    moving[0].send()
    rings[3].take()
    moving[2].take()
    rings[2] = ring(moving[2])
    rings[2].send()
    rings[3].send()
    rings[1].take()
    moving[1] = onward(moving[1], rings[1].blocks)
    moving[1].send()
    moving[0].take()
    moving[0].send()
    rings[2].take()
    rings[2].send()
    rings[3].take()
    rings[3].send()
    moving[1].take()
    rings[2].take()
    rings[2].send()
    moving[1].send()
    moving[0].take()
    moving[0].send()
    rings[3].take()
    out = times(rings[3].blocks, None, 6 * TILE, SLOTS * TILE)
    rings[2].take()
    out = times(rings[2].blocks, out, 4 * TILE, SLOTS * TILE)
    moving[1].take()
    moving[0].take()
    out = lax.dynamic_update_slice(out, moving[0].value.reshape(-1, WIDTH), (0 * TILE, 0))
    out = lax.dynamic_update_slice(out, moving[1].value.reshape(-1, WIDTH), (2 * TILE, 0))
    return out


def solution(mesh):
    placed = (P("row", "col"), P("row", "col"), P("row", "col"), P())
    return jax.shard_map(
        body, mesh=mesh, in_specs=placed, out_specs=P("row", "col"), check_vma=False
    )
```

```python
import functools

import jax
import jax.numpy as jnp
import numpy as np
from jax import lax
from jax.experimental import pallas as pl
from jax.experimental.pallas import tpu as pltpu
from jax.sharding import PartitionSpec as P

TILE = 128
SLOTS = 8
DEPTH = 1024
WIDTH = 1536
CORE = (1, 1)
X_A, X_B, Y_A, Y_B = (2, 6), (6, 2), (8, 24), (24, 8)
STEPS = (CORE, X_A, X_B, Y_A, Y_B)
FUNCTIONAL = {1: 1, 2: 6, 6: 4, 8: 24, 24: 16}
GATHER = (X_A, X_B, Y_A, Y_B)
AXES = ("row", "col")


def exchange(value, masks):
    pairs = [(p, p ^ masks[p & 1]) for p in range(lax.axis_size("row"))]
    return lax.ppermute(value, "row", pairs)


def turn(value):
    rows, cols = lax.axis_size("row"), lax.axis_size("col")
    pairs = []
    for p in range(rows):
        step = 1 if p & 1 == 0 else -1
        for c in range(cols):
            pairs.append((p * cols + c, p * cols + (c + step) % cols))
    return lax.ppermute(value, AXES, pairs)


def choose(flags, masks, low, high, partner, mine):
    taken = flags[STEPS.index(masks), low:high] == 1
    return jnp.where(taken[:, None, None], partner, mine)


def pack_kernel(screen_ref, amplitudes_ref, out_ref):
    first = jnp.int32(11)
    second = jnp.int32(0)
    for j in range(12):
        live = screen_ref[0, j] == 1
        first = jnp.where(live, jnp.minimum(first, j), first)
        second = jnp.where(live, jnp.maximum(second, j), second)
    one = amplitudes_ref[:, pl.ds(pl.multiple_of(first * TILE, TILE), TILE)]
    two = amplitudes_ref[:, pl.ds(pl.multiple_of(second * TILE, TILE), TILE)]
    out_ref[0, :TILE, :TILE] = one
    out_ref[0, :TILE, TILE:] = jnp.where(first != second, two, jnp.zeros_like(two))
    side = lax.broadcasted_iota(jnp.int32, (16, 2 * TILE), 1) < TILE
    out_ref[0, TILE:, :] = jnp.where(side, first, second).astype(jnp.float32).astype(jnp.bfloat16)


def pack(amplitudes, screen):
    return pl.pallas_call(
        pack_kernel,
        in_specs=[pl.BlockSpec(memory_space=pltpu.SMEM), pl.BlockSpec(memory_space=pltpu.VMEM)],
        out_specs=pl.BlockSpec(memory_space=pltpu.VMEM),
        out_shape=jax.ShapeDtypeStruct((1, TILE + 16, 2 * TILE), jnp.bfloat16),
        cost_estimate=pl.CostEstimate(flops=1, bytes_accessed=1, transcendentals=0),
    )(screen, amplitudes)


def order_table():
    table = np.zeros((32, 32), np.int32)
    for me in range(32):
        for k in range(32):
            delta = k ^ me
            at = 16 * (delta & 1)
            for i, masks in enumerate(GATHER):
                at += (bin(delta & FUNCTIONAL[masks[k & 1]]).count("1") & 1) << i
            table[me, k] = at
    return table


def product_kernel(first, at_ref, place_ref, base_ref, *refs):
    *sources, tiles_hbm = refs[:5]
    out_hbm, x, tiles, total, out, sems = refs[-6:]
    rows = out.shape[0]
    loads = [pltpu.make_async_copy(tiles_hbm, tiles, sems.at[4])]
    loads += [pltpu.make_async_copy(sources[j], x.at[j], sems.at[j]) for j in range(4)]
    for load in loads:
        load.start()
    total[...] = jnp.zeros_like(total)
    loads[0].wait()
    for j in range(4):
        loads[j + 1].wait()

        for kk in range(8):
            at = at_ref[0, base_ref[j] * 8 + kk]
            part = jnp.dot(
                x[j, :, kk * TILE : (kk + 1) * TILE],
                tiles[at, :TILE, :],
                preferred_element_type=jnp.float32,
            )
            for i in range(2):
                total[place_ref[2 * at + i]] += part[:, i * TILE : (i + 1) * TILE]

    for j in range(WIDTH // TILE):
        out[:, j * TILE : (j + 1) * TILE] = total[j].astype(out.dtype)
    store = pltpu.make_async_copy(out, out_hbm.at[pl.ds(first, rows)], sems.at[5])
    store.start()
    store.wait()


def product(blocks, tiles, at, place, base, out=None, first=0, rows_all=None):
    rows = blocks[0].shape[0]
    rows_all = rows_all or rows
    args = list(blocks) + [tiles]
    aliases = {}
    if out is not None:
        args.append(out)
        aliases = {8: 0}
    return pl.pallas_call(
        functools.partial(product_kernel, first),
        grid_spec=pltpu.PrefetchScalarGridSpec(
            num_scalar_prefetch=3,
            grid=(1,),
            in_specs=[pl.BlockSpec(memory_space=pl.ANY)] * len(args),
            out_specs=pl.BlockSpec(memory_space=pl.ANY),
            scratch_shapes=[
                pltpu.VMEM((4, rows, DEPTH), jnp.bfloat16),
                pltpu.VMEM(tiles.shape, jnp.bfloat16),
                pltpu.VMEM((WIDTH // TILE, rows, TILE), jnp.float32),
                pltpu.VMEM((rows, WIDTH), jnp.bfloat16),
                pltpu.SemaphoreType.DMA((6,)),
            ],
        ),
        out_shape=jax.ShapeDtypeStruct((rows_all, WIDTH), jnp.bfloat16),
        input_output_aliases=aliases,
        compiler_params=pltpu.CompilerParams(vmem_limit_bytes=16 * 2**20),
        cost_estimate=pl.CostEstimate(flops=1, bytes_accessed=1, transcendentals=0),
    )(at, place, base, *args)


class Sequence:
    def __init__(self, token):
        self.token = token

    def tied(self, *values):
        return lax.optimization_barrier((*values, self.token))[: len(values)]

    def after(self, value):
        return self.tied(value)[0]

    def done(self, value):
        self.token = self.after(value)
        return self.token


SPANS = ((0, 2), (2, 4), (4, 6), (6, 8))
PATHS = (
    (Y_A, Y_B, X_A, X_B),
    (X_A, X_B, Y_A, Y_B),
    (X_A, Y_A, Y_B, X_B),
    (Y_A, Y_B, X_A, X_B),
)


def body(integrals, amplitudes, screen, next_owner):
    me = lax.axis_index("row").astype(jnp.int32)
    col = lax.axis_index("col").astype(jnp.int32)
    core = me & 1
    slots = integrals.reshape(SLOTS, TILE, DEPTH)

    functional = [jnp.asarray([[FUNCTIONAL[m[c]]] for m in STEPS], jnp.int32) for c in range(2)]
    value = next_owner[None, :SLOTS] & jnp.where(core == 0, functional[0], functional[1])
    value = value ^ value >> 4
    value = value ^ value >> 2
    value = value ^ value >> 1
    flags = value & 1
    at = lax.dynamic_slice(jnp.asarray(order_table()), (me, 0), (1, 32))
    sign = 1 - 2 * core
    base = (col - sign * jnp.arange(4, dtype=jnp.int32)) & 3
    flags, at, base = lax.optimization_barrier((flags, at, base))

    seq = Sequence(next_owner)

    class Moving:
        def __init__(self, value, cut, order):
            self.value, self.cut, self.order, self.at = value, cut, order, 0

        def send(self):
            self.value = seq.after(self.value)
            self.partner = exchange(self.value, self.order[self.at])

        def take(self):
            partner, mine = seq.tied(self.partner, self.value)
            self.value = seq.done(choose(flags, self.order[self.at], *self.cut, partner, mine))
            self.at += 1

    class Ring:
        def __init__(self, value):
            self.blocks = [value]

        def send(self):
            self.blocks.append(turn(seq.after(self.blocks[-1])))

        def take(self):
            self.blocks[-1] = seq.done(self.blocks[-1])

    class Tiles:
        def __init__(self, value):
            self.value, self.at = value, 0

        def send(self):
            self.value = seq.after(self.value)
            self.partner = exchange(self.value, (*GATHER, CORE)[self.at])
            self.at += 1

        def take(self):
            partner, mine = seq.tied(self.partner, self.value)
            self.value = seq.done(jnp.concatenate([mine, partner], axis=0))

    swapped = exchange(slots, CORE)

    def group(number):
        low, high = SPANS[number]
        other, mine = seq.tied(swapped, slots)
        value = seq.done(choose(flags, CORE, low, high, other[low:high], mine[low:high]))
        return Moving(value, SPANS[number], PATHS[number])

    def ring(moving):
        return Ring(moving.value.reshape(-1, DEPTH))

    def times(blocks, *place_in):
        live = tiles.value
        place = live[:, TILE, :].reshape(32, 2, TILE)[:, :, 0].astype(jnp.int32).reshape(64)
        return seq.done(product(blocks, live, at, place, base, *place_in))

    def onward(moving, blocks):
        value = times(blocks).reshape(-1, TILE, WIDTH)
        later = Moving(value, moving.cut, moving.order)
        later.at = moving.at
        return later

    moving, rings = [None] * 4, [None] * 4
    tiles = Tiles(seq.done(pack(amplitudes, screen)))
    tiles.send()
    moving[3] = group(3)
    moving[3].send()
    moving[0] = group(0)
    tiles.take()
    tiles.send()
    moving[1] = group(1)
    moving[1].send()
    rings[0] = ring(moving[0])
    rings[0].send()
    moving[2] = group(2)
    moving[2].send()
    rings[0].take()
    tiles.take()
    tiles.send()
    moving[3].take()
    moving[3].send()
    moving[1].take()
    moving[1].send()
    rings[0].send()
    tiles.take()
    tiles.send()
    moving[2].take()
    moving[2].send()
    moving[3].take()
    moving[3].send()
    moving[1].take()
    rings[0].take()
    rings[0].send()
    rings[1] = ring(moving[1])
    rings[1].send()
    tiles.take()
    tiles.send()
    moving[3].take()
    moving[3].send()
    tiles.take()
    moving[2].take()
    moving[2].send()
    rings[0].take()
    rings[1].take()
    moving[0] = onward(moving[0], rings[0].blocks)
    moving[0].send()
    rings[1].send()
    moving[3].take()
    rings[3] = ring(moving[3])
    rings[3].send()
    moving[2].take()
    moving[2].send()
    rings[1].take()
    rings[1].send()
    moving[0].take()
    moving[0].send()
    rings[3].take()
    moving[2].take()
    rings[2] = ring(moving[2])
    rings[2].send()
    rings[3].send()
    rings[1].take()
    rings[2].take()
    moving[1] = onward(moving[1], rings[1].blocks)
    moving[1].send()
    moving[0].take()
    moving[0].send()
    rings[2].send()
    rings[3].take()
    rings[3].send()
    moving[1].take()
    rings[2].take()
    rings[2].send()
    moving[1].send()
    moving[0].take()
    moving[0].send()
    rings[3].take()
    out = times(rings[3].blocks, None, 6 * TILE, SLOTS * TILE)
    rings[2].take()
    out = times(rings[2].blocks, out, 4 * TILE, SLOTS * TILE)
    moving[1].take()
    moving[0].take()
    out = lax.dynamic_update_slice(out, moving[0].value.reshape(-1, WIDTH), (0 * TILE, 0))
    out = lax.dynamic_update_slice(out, moving[1].value.reshape(-1, WIDTH), (2 * TILE, 0))
    return out


def solution(mesh):
    placed = (P("row", "col"), P("row", "col"), P("row", "col"), P())
    return jax.shard_map(
        body, mesh=mesh, in_specs=placed, out_specs=P("row", "col"), check_vma=False
    )
```

```python
import functools

import jax
import jax.numpy as jnp
import numpy as np
from jax import lax
from jax.experimental import pallas as pl
from jax.experimental.pallas import tpu as pltpu
from jax.sharding import PartitionSpec as P

TILE = 128
SLOTS = 8
DEPTH = 1024
WIDTH = 1536
CORE = (1, 1)
X_A, X_B, Y_A, Y_B = (2, 6), (6, 2), (8, 24), (24, 8)
STEPS = (CORE, X_A, X_B, Y_A, Y_B)
FUNCTIONAL = {1: 1, 2: 6, 6: 4, 8: 24, 24: 16}
GATHER = (X_A, X_B, Y_A, Y_B)
AXES = ("row", "col")


def exchange(value, masks):
    pairs = [(p, p ^ masks[p & 1]) for p in range(lax.axis_size("row"))]
    return lax.ppermute(value, "row", pairs)


def turn(value):
    rows, cols = lax.axis_size("row"), lax.axis_size("col")
    pairs = []
    for p in range(rows):
        step = 1 if p & 1 == 0 else -1
        for c in range(cols):
            pairs.append((p * cols + c, p * cols + (c + step) % cols))
    return lax.ppermute(value, AXES, pairs)


def choose(flags, masks, low, high, partner, mine):
    taken = flags[STEPS.index(masks), low:high] == 1
    return jnp.where(taken[:, None, None], partner, mine)


def pack_kernel(screen_ref, amplitudes_ref, out_ref):
    first = jnp.int32(11)
    second = jnp.int32(0)
    for j in range(12):
        live = screen_ref[0, j] == 1
        first = jnp.where(live, jnp.minimum(first, j), first)
        second = jnp.where(live, jnp.maximum(second, j), second)
    one = amplitudes_ref[:, pl.ds(pl.multiple_of(first * TILE, TILE), TILE)]
    two = amplitudes_ref[:, pl.ds(pl.multiple_of(second * TILE, TILE), TILE)]
    out_ref[0, :TILE, :TILE] = one
    out_ref[0, :TILE, TILE:] = jnp.where(first != second, two, jnp.zeros_like(two))
    side = lax.broadcasted_iota(jnp.int32, (16, 2 * TILE), 1) < TILE
    out_ref[0, TILE:, :] = jnp.where(side, first, second).astype(jnp.float32).astype(jnp.bfloat16)


def pack(amplitudes, screen):
    return pl.pallas_call(
        pack_kernel,
        in_specs=[pl.BlockSpec(memory_space=pltpu.SMEM), pl.BlockSpec(memory_space=pltpu.VMEM)],
        out_specs=pl.BlockSpec(memory_space=pltpu.VMEM),
        out_shape=jax.ShapeDtypeStruct((1, TILE + 16, 2 * TILE), jnp.bfloat16),
        cost_estimate=pl.CostEstimate(flops=1, bytes_accessed=1, transcendentals=0),
    )(screen, amplitudes)


def order_table():
    table = np.zeros((32, 32), np.int32)
    for me in range(32):
        for k in range(32):
            delta = k ^ me
            at = 16 * (delta & 1)
            for i, masks in enumerate(GATHER):
                at += (bin(delta & FUNCTIONAL[masks[k & 1]]).count("1") & 1) << i
            table[me, k] = at
    return table


def product_kernel(first, at_ref, place_ref, base_ref, *refs):
    *sources, tiles_hbm = refs[:5]
    out_hbm, x, tiles, total, out, sems = refs[-6:]
    rows = out.shape[0]
    loads = [pltpu.make_async_copy(tiles_hbm, tiles, sems.at[4])]
    loads += [pltpu.make_async_copy(sources[j], x.at[j], sems.at[j]) for j in range(4)]
    for load in loads:
        load.start()
    total[...] = jnp.zeros_like(total)
    loads[0].wait()
    for j in range(4):
        loads[j + 1].wait()

        for kk in range(8):
            at = at_ref[0, base_ref[j] * 8 + kk]
            part = jnp.dot(
                x[j, :, kk * TILE : (kk + 1) * TILE],
                tiles[at, :TILE, :],
                preferred_element_type=jnp.float32,
            )
            for i in range(2):
                total[place_ref[2 * at + i]] += part[:, i * TILE : (i + 1) * TILE]

    for j in range(WIDTH // TILE):
        out[:, j * TILE : (j + 1) * TILE] = total[j].astype(out.dtype)
    store = pltpu.make_async_copy(out, out_hbm.at[pl.ds(first, rows)], sems.at[5])
    store.start()
    store.wait()


def product(blocks, tiles, at, place, base, out=None, first=0, rows_all=None):
    rows = blocks[0].shape[0]
    rows_all = rows_all or rows
    args = list(blocks) + [tiles]
    aliases = {}
    if out is not None:
        args.append(out)
        aliases = {8: 0}
    return pl.pallas_call(
        functools.partial(product_kernel, first),
        grid_spec=pltpu.PrefetchScalarGridSpec(
            num_scalar_prefetch=3,
            grid=(1,),
            in_specs=[pl.BlockSpec(memory_space=pl.ANY)] * len(args),
            out_specs=pl.BlockSpec(memory_space=pl.ANY),
            scratch_shapes=[
                pltpu.VMEM((4, rows, DEPTH), jnp.bfloat16),
                pltpu.VMEM(tiles.shape, jnp.bfloat16),
                pltpu.VMEM((WIDTH // TILE, rows, TILE), jnp.float32),
                pltpu.VMEM((rows, WIDTH), jnp.bfloat16),
                pltpu.SemaphoreType.DMA((6,)),
            ],
        ),
        out_shape=jax.ShapeDtypeStruct((rows_all, WIDTH), jnp.bfloat16),
        input_output_aliases=aliases,
        compiler_params=pltpu.CompilerParams(vmem_limit_bytes=16 * 2**20),
        cost_estimate=pl.CostEstimate(flops=1, bytes_accessed=1, transcendentals=0),
    )(at, place, base, *args)


class Sequence:
    def __init__(self, token):
        self.token = token

    def tied(self, *values):
        return lax.optimization_barrier((*values, self.token))[: len(values)]

    def after(self, value):
        return self.tied(value)[0]

    def done(self, value):
        self.token = self.after(value)
        return self.token


SPANS = ((0, 2), (2, 4), (4, 6), (6, 8))
PATHS = (
    (Y_A, Y_B, X_A, X_B),
    (X_A, X_B, Y_A, Y_B),
    (X_A, Y_A, X_B, Y_B),
    (Y_A, Y_B, X_A, X_B),
)


def body(integrals, amplitudes, screen, next_owner):
    me = lax.axis_index("row").astype(jnp.int32)
    col = lax.axis_index("col").astype(jnp.int32)
    core = me & 1
    slots = integrals.reshape(SLOTS, TILE, DEPTH)

    functional = [jnp.asarray([[FUNCTIONAL[m[c]]] for m in STEPS], jnp.int32) for c in range(2)]
    value = next_owner[None, :SLOTS] & jnp.where(core == 0, functional[0], functional[1])
    value = value ^ value >> 4
    value = value ^ value >> 2
    value = value ^ value >> 1
    flags = value & 1
    at = lax.dynamic_slice(jnp.asarray(order_table()), (me, 0), (1, 32))
    sign = 1 - 2 * core
    base = (col - sign * jnp.arange(4, dtype=jnp.int32)) & 3
    flags, at, base = lax.optimization_barrier((flags, at, base))

    seq = Sequence(next_owner)

    class Moving:
        def __init__(self, value, cut, order):
            self.value, self.cut, self.order, self.at = value, cut, order, 0

        def send(self):
            self.value = seq.after(self.value)
            self.partner = exchange(self.value, self.order[self.at])

        def take(self):
            partner, mine = seq.tied(self.partner, self.value)
            self.value = seq.done(choose(flags, self.order[self.at], *self.cut, partner, mine))
            self.at += 1

    class Ring:
        def __init__(self, value):
            self.blocks = [value]

        def send(self):
            self.blocks.append(turn(seq.after(self.blocks[-1])))

        def take(self):
            self.blocks[-1] = seq.done(self.blocks[-1])

    class Tiles:
        def __init__(self, value):
            self.value, self.at = value, 0

        def send(self):
            self.value = seq.after(self.value)
            self.partner = exchange(self.value, (*GATHER, CORE)[self.at])
            self.at += 1

        def take(self):
            partner, mine = seq.tied(self.partner, self.value)
            self.value = seq.done(jnp.concatenate([mine, partner], axis=0))

    swapped = exchange(slots, CORE)

    def group(number):
        low, high = SPANS[number]
        other, mine = seq.tied(swapped, slots)
        value = seq.done(choose(flags, CORE, low, high, other[low:high], mine[low:high]))
        return Moving(value, SPANS[number], PATHS[number])

    def ring(moving):
        return Ring(moving.value.reshape(-1, DEPTH))

    def times(blocks, *place_in):
        live = tiles.value
        place = live[:, TILE, :].reshape(32, 2, TILE)[:, :, 0].astype(jnp.int32).reshape(64)
        return seq.done(product(blocks, live, at, place, base, *place_in))

    def onward(moving, blocks):
        value = times(blocks).reshape(-1, TILE, WIDTH)
        later = Moving(value, moving.cut, moving.order)
        later.at = moving.at
        return later

    moving, rings = [None] * 4, [None] * 4
    tiles = Tiles(seq.done(pack(amplitudes, screen)))
    tiles.send()
    moving[3] = group(3)
    moving[3].send()
    moving[0] = group(0)
    tiles.take()
    tiles.send()
    moving[1] = group(1)
    moving[1].send()
    rings[0] = ring(moving[0])
    rings[0].send()
    moving[2] = group(2)
    moving[2].send()
    rings[0].take()
    tiles.take()
    tiles.send()
    moving[3].take()
    moving[3].send()
    moving[1].take()
    moving[1].send()
    rings[0].send()
    tiles.take()
    tiles.send()
    moving[2].take()
    moving[2].send()
    moving[3].take()
    moving[3].send()
    moving[1].take()
    rings[0].take()
    rings[0].send()
    rings[1] = ring(moving[1])
    rings[1].send()
    tiles.take()
    tiles.send()
    moving[3].take()
    moving[3].send()
    tiles.take()
    moving[2].take()
    rings[0].take()
    moving[2].send()
    rings[1].take()
    moving[0] = onward(moving[0], rings[0].blocks)
    moving[0].send()
    rings[1].send()
    moving[3].take()
    rings[3] = ring(moving[3])
    rings[3].send()
    moving[2].take()
    moving[2].send()
    rings[1].take()
    rings[1].send()
    moving[0].take()
    moving[0].send()
    moving[2].take()
    rings[3].take()
    rings[2] = ring(moving[2])
    rings[2].send()
    rings[3].send()
    rings[1].take()
    rings[2].take()
    moving[1] = onward(moving[1], rings[1].blocks)
    moving[1].send()
    moving[0].take()
    moving[0].send()
    rings[2].send()
    rings[3].take()
    rings[3].send()
    moving[1].take()
    rings[2].take()
    rings[2].send()
    moving[1].send()
    moving[0].take()
    moving[0].send()
    rings[3].take()
    out = times(rings[3].blocks, None, 6 * TILE, SLOTS * TILE)
    rings[2].take()
    out = times(rings[2].blocks, out, 4 * TILE, SLOTS * TILE)
    moving[1].take()
    moving[0].take()
    out = lax.dynamic_update_slice(out, moving[0].value.reshape(-1, WIDTH), (0 * TILE, 0))
    out = lax.dynamic_update_slice(out, moving[1].value.reshape(-1, WIDTH), (2 * TILE, 0))
    return out


def solution(mesh):
    placed = (P("row", "col"), P("row", "col"), P("row", "col"), P())
    return jax.shard_map(
        body, mesh=mesh, in_specs=placed, out_specs=P("row", "col"), check_vma=False
    )
```
